32 devices in a mesh: dp: 4 (over y, x), tensor: 8 (over z, core).
Axes of the slice: x: 2, y: 2, z: 4, core: 2. Of those that a mesh axis runs over, the one named last changes fastest.
Arguments:
- query_states: bfloat16 [1536, 4096], P('dp', 'tensor'), may hold values from -64 to 64
- key_states: bfloat16 [1536, 4096], P('dp', 'tensor'), may hold values from -12 to 12
- value_states: bfloat16 [1536, 4096], P('dp', 'tensor'), may hold values from -6 to 6
- residual: bfloat16 [1536, 4096], P('dp', 'tensor'), may hold values from -6 to 6
- norm_gains: float32 [4, 4096], replicated, may hold values from 0.1 to 1.9
- lang_labels: int32 [32], replicated, may hold values from 0 to 3
- doc_lengths: int32 [32, 4], replicated, may hold values from 1 to 32, 48 in all within a row
- destinations: int32 [32], replicated, may hold values from 0 to 3, as said below
- gate_weight: bfloat16 [4096, 14336], P(None, 'tensor'), may hold values from -0.09375 to 0.09375
- up_weight: bfloat16 [4096, 14336], P(None, 'tensor'), may hold values from -0.09375 to 0.09375
- down_weight: bfloat16 [14336, 4096], P('tensor'), may hold values from -0.046875 to 0.046875
- out_cotangent: bfloat16 [1536, 4096], P(('dp', 'tensor')), may hold values from -6 to 6
Outputs:
- layer_out: bfloat16 [1536, 4096], P(('dp', 'tensor'))
- input_grad: bfloat16 [1536, 4096], P(('dp', 'tensor'))
- gate_grad: bfloat16 [4096, 14336], P('dp', 'tensor')
- up_grad: bfloat16 [4096, 14336], P('dp', 'tensor')
- down_grad: bfloat16 [14336, 4096], P('tensor', 'dp')
The draws below stay inside these ranges and needn't reach their ends.
Inputs may be any that keep to these rules, and one draw needn't show every extreme that they name: `destinations`: every data group receives exactly 8 units. One group sends at most 2 units to any one group, and every group sends exactly 2 units to some group.
All inputs are finite; a program needn't handle non-finite values.
Results may differ from the reference program's by a relative error of at most 0.015.
Values may be sent and summed in bfloat16 or wider, within the bound.
A program may use at most 192 MiB of HBM per device.

```python
import math
import jax
import jax.numpy as jnp
import numpy as np
from jax import lax

D = 4096
FF = 14336
HEADS = 32
HD = 128
UNIT = 48
UNITS = 8
CAP = 2
NDOC = 4
NLANG = 4
MOST = 32
WIN = 24
TOK_GRP = 384
NUNITS = 32
TOK_ALL = 1536
N_DP = 4


def drawn_pair(key):
    base_key = jax.random.fold_in(key, 101)
    key_noise, query_noise = jax.random.split(base_key, 2)
    array_shape = (TOK_ALL, D)
    keys_drawn = jnp.clip(jax.random.normal(key_noise, array_shape, jnp.float32), -6.0, 6.0)
    queries_drawn = jnp.clip(jax.random.normal(query_noise, array_shape, jnp.float32), -6.0, 6.0)
    queries = queries_drawn
    keys_out = keys_drawn
    return (jnp.clip(queries, -64.0, 64.0), jnp.clip(keys_out, -12.0, 12.0))


def draw_query_states(key, part):
    return drawn_pair(key)[0].astype(jnp.bfloat16)


def draw_key_states(key, part):
    return drawn_pair(key)[1].astype(jnp.bfloat16)


def draw_destinations(key, part):
    base_key = jax.random.fold_in(key, 202)
    offset_key, shuffle_key = jax.random.split(base_key)
    shuffled = jax.random.permutation(offset_key, N_DP)
    offsets = shuffled[jnp.arange(UNITS) // CAP]

    def per_group(group_index):
        unit_order = jax.random.permutation(jax.random.fold_in(shuffle_key, group_index), UNITS)
        return (group_index + offsets[unit_order]) % N_DP
    return jax.vmap(per_group)(jnp.arange(N_DP, dtype=jnp.int32)).reshape(-1).astype(jnp.int32)


def place_ends(values, rng, least, top_value):
    index_at = [jax.random.randint(jax.random.fold_in(rng, axis), (), 0, length) for axis, length in enumerate(values.shape)]
    widest = values.shape.index(max(values.shape))
    beside = index_at[:widest] + [(index_at[widest] + 1) % values.shape[widest]] + index_at[widest + 1:]
    return values.at[tuple(index_at)].set(least).at[tuple(beside)].set(top_value)


def block_levels(own_key, extent, cuts, low, largest):
    loudness = 1.0
    for axis_at, blocks in cuts:
        draws = jax.random.uniform(jax.random.fold_in(jax.random.fold_in(own_key, 6), axis_at), (blocks,), jnp.float32, low / len(cuts), largest / len(cuts))
        loudness = loudness * jnp.repeat(jnp.exp(draws), extent[axis_at] // blocks).reshape((-1,) + (1,) * (len(extent) - 1 - axis_at))
    return loudness


def profile(number_of, total, bound, lean):
    weights = [(1 << 20) // math.isqrt(grade ** lean) + 1 for grade in range(2, number_of + 1)]
    surplus, counts = total - bound - (number_of - 1), [1] * (number_of - 1)
    while surplus > 0:
        movable = [i for i in range(number_of - 1) if counts[i] < bound]
        mass, budget = sum([weights[i] for i in movable]), surplus
        for i in movable:
            more = min(bound - counts[i], max(1, budget * weights[i] // mass), surplus)
            counts[i] = counts[i] + more
            surplus = surplus - more
    return np.array([bound] + counts)


def uneven(rng, count, total, bound, skew):
    if count == 2:
        one = jax.random.randint(rng, (), max(1, total - bound), min(bound, total - 1) + 1)
        return jnp.stack([one, total - one])
    tallies = jnp.asarray(profile(count, total, bound, skew), jnp.int32)
    twos = (count - 1) // 2
    source_of, receiver = tallies[1:1 + 2 * twos:2], tallies[2:2 + 2 * twos:2]
    slack = jnp.minimum(source_of - 1, bound - receiver)
    moved = jax.random.randint(jax.random.fold_in(rng, 1), (twos,), 0, 1 << 20) % (slack + 1)
    tallies = tallies.at[1:1 + 2 * twos:2].set(source_of - moved).at[2:2 + 2 * twos:2].set(receiver + moved)
    return tallies[jax.random.permutation(jax.random.fold_in(rng, 2), count)]


def gaussian(stream_key, shape, width, most, cuts=(), kind=jnp.bfloat16):
    result = width * jax.random.normal(stream_key, shape, jnp.float32)
    if cuts:
        result = result * block_levels(stream_key, shape, cuts, -0.22, 0.18)
    return jnp.clip(result, -most, most).astype(kind)


def setup_inputs(seed: int = 0) -> dict:
    arg_keys = jax.random.split(jax.random.key(seed), 13)
    return {
        "query_states": draw_query_states(jax.random.fold_in(arg_keys[12], 71), 0),
        "key_states": draw_key_states(jax.random.fold_in(arg_keys[12], 71), 0),
        "value_states": gaussian(arg_keys[2], (TOK_ALL, D), 1.0, 6.0, ((0, 4), (1, 8))),
        "residual": gaussian(arg_keys[3], (TOK_ALL, D), 1.0, 6.0, ((0, 4), (1, 8))),
        "norm_gains": jnp.clip(1.0 + 0.18 * jax.random.normal(arg_keys[4], (NLANG, D), jnp.float32), 0.1, 1.9),
        "lang_labels": place_ends(jax.random.randint(arg_keys[5], (NUNITS,), 0, NLANG), jax.random.fold_in(arg_keys[5], 1), 0, NLANG - 1).astype(jnp.int32),
        "doc_lengths": jax.vmap(lambda own: uneven(own, NDOC, UNIT, MOST, 2))(jax.random.split(arg_keys[6], NUNITS)).reshape((NUNITS, NDOC)).astype(jnp.int32),
        "destinations": draw_destinations(jax.random.fold_in(arg_keys[12], 71), 0),
        "gate_weight": gaussian(arg_keys[8], (D, FF), D ** -0.5, 0.09375, ((1, 8),)),
        "up_weight": gaussian(arg_keys[9], (D, FF), D ** -0.5, 0.09375, ((1, 8),)),
        "down_weight": gaussian(arg_keys[10], (FF, D), FF ** -0.5, 0.046875, ((0, 8),)),
        "out_cotangent": gaussian(arg_keys[11], (TOK_ALL, D), 1.0, 6.0, ((0, 32),)),
    }


def doc_index(doc_lengths):
    doc_ends = jnp.cumsum(doc_lengths, axis=1)
    positions = jnp.arange(UNIT, dtype=jnp.int32)
    return lax.optimization_barrier(jnp.sum((doc_ends[:, None, :] <= positions[None, :, None]).astype(jnp.int32), axis=2))

def attend(query_units, key_units, value_units, resid_units, doc_units):
    unit_count = query_units.shape[0]
    head_shape = (unit_count, UNIT, HEADS, HD)
    query_heads = query_units.reshape(head_shape).astype(jnp.float32)
    key_heads = key_units.reshape(head_shape).astype(jnp.float32)
    value_heads = value_units.reshape(head_shape).astype(jnp.float32)
    scores = jnp.einsum('uqhd,ukhd->uhqk', query_heads, key_heads) / math.sqrt(HD)
    positions = jnp.arange(UNIT, dtype=jnp.int32)
    distance = positions[:, None] - positions[None, :]
    allowed = (doc_units[:, :, None] == doc_units[:, None, :]) & ((distance >= 0) & (distance < WIN))[None]
    scores = jnp.where(allowed[:, None], scores, -1e+30)
    row_max = lax.optimization_barrier(jnp.max(scores, axis=3, keepdims=True))
    exp_scores = jnp.exp(scores - row_max)
    attn_probs = (exp_scores / lax.optimization_barrier(jnp.sum(exp_scores, axis=3, keepdims=True))).astype(jnp.bfloat16)
    mixed_heads = jnp.einsum('uhqk,ukhd->uqhd', attn_probs.astype(jnp.float32), value_heads)
    return (resid_units.astype(jnp.float32) + mixed_heads.reshape(unit_count, UNIT, D)).astype(jnp.bfloat16)

def reference(query_states, key_states, value_states, residual, norm_gains, lang_labels, doc_lengths, destinations, gate_weight, up_weight, down_weight, out_cotangent):
    unit_shape = (NUNITS, UNIT, D)
    doc_ids = doc_index(doc_lengths)
    mixed = attend(query_states.reshape(unit_shape), key_states.reshape(unit_shape), value_states.reshape(unit_shape), residual.reshape(unit_shape), doc_ids)
    unit_order = jnp.argsort(destinations, stable=True).astype(jnp.int32)
    stream = mixed[unit_order].reshape(TOK_ALL, D)
    lang_units = lang_labels[unit_order]
    gain_tokens = jnp.repeat(norm_gains[lang_units], UNIT, axis=0)
    stream_f = stream.astype(jnp.float32)
    scaled = (stream_f * gain_tokens).astype(jnp.bfloat16)
    inv_rms = lax.rsqrt(lax.optimization_barrier(jnp.sum(stream_f * stream_f, axis=1)) / D + 1e-05)
    act_gate = inv_rms[:, None] * jnp.dot(scaled, gate_weight, preferred_element_type=jnp.float32)
    act_up = inv_rms[:, None] * jnp.dot(scaled, up_weight, preferred_element_type=jnp.float32)
    hidden = (jax.nn.silu(act_gate) * act_up).astype(jnp.bfloat16)
    layer_out = (stream_f + jnp.dot(hidden, down_weight, preferred_element_type=jnp.float32)).astype(jnp.bfloat16)
    grad_hidden = jnp.dot(out_cotangent, down_weight.T, preferred_element_type=jnp.float32)
    sigma = jax.nn.sigmoid(act_gate)
    grad_gate = (inv_rms[:, None] * grad_hidden * act_up * sigma * (1.0 + act_gate * (1.0 - sigma))).astype(jnp.bfloat16)
    grad_up = (inv_rms[:, None] * grad_hidden * jax.nn.silu(act_gate)).astype(jnp.bfloat16)
    back = jnp.dot(grad_gate, gate_weight.T, preferred_element_type=jnp.float32) + jnp.dot(grad_up, up_weight.T, preferred_element_type=jnp.float32)
    dot_sum = lax.optimization_barrier(jnp.sum(scaled.astype(jnp.float32) * back, axis=1))
    input_grad = (out_cotangent.astype(jnp.float32) + gain_tokens * back - (inv_rms * inv_rms / D)[:, None] * stream_f * dot_sum[:, None]).astype(jnp.bfloat16)
    factors = jnp.concatenate([grad_gate, grad_up], axis=1)

    def group_terms(totals, group_index):
        row_start = group_index * TOK_GRP
        scaled_rows = lax.dynamic_slice_in_dim(scaled, row_start, TOK_GRP, 0)
        factor_rows = lax.dynamic_slice_in_dim(factors, row_start, TOK_GRP, 0)
        hidden_rows = lax.dynamic_slice_in_dim(hidden, row_start, TOK_GRP, 0)
        cot_rows = lax.dynamic_slice_in_dim(out_cotangent, row_start, TOK_GRP, 0)
        gate_up_part = jnp.dot(scaled_rows.T, factor_rows, preferred_element_type=jnp.float32).astype(jnp.bfloat16)
        down_part = jnp.dot(cot_rows.T, hidden_rows, preferred_element_type=jnp.float32).astype(jnp.bfloat16)
        gate_up_part, down_part = lax.optimization_barrier((gate_up_part, down_part))
        return ((totals[0] + gate_up_part.astype(jnp.float32), totals[1] + down_part.astype(jnp.float32)), None)
    start_totals = (jnp.zeros((D, 2 * FF), jnp.float32), jnp.zeros((D, FF), jnp.float32))
    group_ids = jnp.arange(N_DP, dtype=jnp.int32)
    totals, unused = lax.scan(group_terms, start_totals, group_ids)
    gate_grad = totals[0][:, :FF].astype(jnp.bfloat16)
    up_grad = totals[0][:, FF:].astype(jnp.bfloat16)
    down_grad = totals[1].T.astype(jnp.bfloat16)
    return (layer_out, input_grad, gate_grad, up_grad, down_grad)
```

```python
import math

import jax
import jax.numpy as jnp
from jax import lax
from jax.sharding import PartitionSpec as P

HD = 128
UNIT = 48
CAP = 2
WIN = 24


def doc_index(doc_lengths, unit_len):
    doc_ends = jnp.cumsum(doc_lengths, axis=1)
    positions = jnp.arange(unit_len, dtype=jnp.int32)
    return jnp.sum((doc_ends[:, None, :] <= positions[None, :, None]).astype(jnp.int32), axis=2)


def attend(query_units, key_units, value_units, resid_units, doc_units):
    unit_count, unit_len, columns = query_units.shape
    head_shape = (unit_count, unit_len, columns // HD, HD)
    scores = jnp.einsum(
        "uqhd,ukhd->uhqk",
        query_units.reshape(head_shape),
        key_units.reshape(head_shape),
        preferred_element_type=jnp.float32,
    ) / math.sqrt(HD)
    positions = jnp.arange(unit_len, dtype=jnp.int32)
    distance = positions[:, None] - positions[None, :]
    allowed = (doc_units[:, :, None] == doc_units[:, None, :]) & (
        (distance >= 0) & (distance < WIN)
    )[None]
    scores = jnp.where(allowed[:, None], scores, -1e30)
    row_max = jnp.max(scores, axis=3, keepdims=True)
    exp_scores = jnp.exp(scores - row_max)
    attn_probs = (exp_scores / jnp.sum(exp_scores, axis=3, keepdims=True)).astype(jnp.bfloat16)
    mixed_heads = jnp.einsum(
        "uhqk,ukhd->uqhd",
        attn_probs,
        value_units.reshape(head_shape),
        preferred_element_type=jnp.float32,
    )
    return (
        resid_units.astype(jnp.float32) + mixed_heads.reshape(unit_count, unit_len, columns)
    ).astype(jnp.bfloat16)


def pack_units(send_table, unit_data):
    return jnp.einsum(
        "tsu,uic->tsic", send_table, unit_data, preferred_element_type=jnp.float32
    ).astype(jnp.bfloat16)


def unpack_units(recv_table, arrived):
    return jnp.einsum(
        "jts,tsic->jic", recv_table, arrived, preferred_element_type=jnp.float32
    ).astype(jnp.bfloat16)


def exchange(block, distance):
    groups = lax.axis_size("dp")
    return lax.ppermute(block, "dp", [(i, i ^ distance) for i in range(groups)])


def first_hops(block):
    groups = lax.axis_size("dp")
    distances = (1, 2) if groups == 4 else range(1, groups)
    return [exchange(block, o) for o in distances]


def second_hops(arrived):
    if lax.axis_size("dp") != 4:
        return []
    half = arrived[0].shape[0] // 2
    return [exchange(arrived[0][:half], 2), exchange(arrived[1][half:], 1)]


def after(value, *earlier):
    return lax.optimization_barrier((value, *earlier))


def deal(block, share):
    groups = lax.axis_size("dp")
    me = lax.axis_index("dp")
    parts = []
    for o in range(groups):
        piece = lax.dynamic_slice_in_dim(block, (me ^ o) * share, share, 1)
        parts.append(piece if o == 0 else exchange(piece, o))
    return parts


def pick_gains(langs, norm_gains):
    gains = jnp.zeros((langs.shape[0], norm_gains.shape[1]), jnp.float32)
    for index in range(norm_gains.shape[0]):
        gains = jnp.where((langs == index)[:, None], norm_gains[index][None, :], gains)
    return gains


def per_device(
    query_states,
    key_states,
    value_states,
    residual,
    norm_gains,
    lang_labels,
    doc_lengths,
    destinations,
    gate_weight,
    up_weight,
    down_weight,
    out_cotangent,
):
    groups = lax.axis_size("dp")
    shards = lax.axis_size("tensor")
    my_group = lax.axis_index("dp")
    total_units = destinations.shape[0]
    per_group = total_units // groups
    columns = query_states.shape[1]
    width_d = gate_weight.shape[0]
    share = width_d // groups
    tok_group = per_group * UNIT
    rows_here = out_cotangent.shape[0]
    first_unit = my_group * per_group

    cot_full = lax.all_gather(out_cotangent, "tensor", axis=0, tiled=True)

    own_docs = doc_index(lax.dynamic_slice_in_dim(doc_lengths, first_unit, per_group), UNIT)
    unit_shape = (per_group, UNIT, columns)
    mixed_units = attend(
        query_states.reshape(unit_shape),
        key_states.reshape(unit_shape),
        value_states.reshape(unit_shape),
        residual.reshape(unit_shape),
        own_docs,
    )

    unit_index = jnp.arange(total_units, dtype=jnp.int32)
    source_group = unit_index // per_group
    earlier = unit_index[None, :] < unit_index[:, None]
    same_target = destinations[None, :] == destinations[:, None]
    same_source = source_group[None, :] == source_group[:, None]
    send_rank = jnp.sum((earlier & same_target & same_source).astype(jnp.int32), axis=1)
    arrival = jnp.sum((earlier & same_target).astype(jnp.int32), axis=1)
    own_targets = lax.dynamic_slice_in_dim(destinations, first_unit, per_group)
    own_ranks = lax.dynamic_slice_in_dim(send_rank, first_unit, per_group)
    group_ids = jnp.arange(groups, dtype=jnp.int32)
    slot_ids = jnp.arange(CAP, dtype=jnp.int32)
    send_table = (
        (own_targets[None, None, :] == group_ids[:, None, None])
        & (own_ranks[None, None, :] == slot_ids[None, :, None])
    ).astype(jnp.bfloat16)
    arrive_ids = jnp.arange(per_group, dtype=jnp.int32)
    landing = (destinations == my_group)[None, :] & (arrival[None, :] == arrive_ids[:, None])
    recv_table = jnp.sum(
        (
            landing[:, None, None, :]
            & (source_group[None, None, None, :] == group_ids[None, :, None, None])
            & (send_rank[None, None, None, :] == slot_ids[None, None, :, None])
        ).astype(jnp.int32),
        axis=3,
    ).astype(jnp.bfloat16)
    moved_langs = jnp.sum(landing.astype(jnp.int32) * lang_labels[None, :], axis=1)
    lang_tokens = jnp.broadcast_to(moved_langs[:, None], (per_group, UNIT)).reshape(tok_group)

    moved = lax.all_to_all(
        pack_units(send_table, mixed_units), "dp", split_axis=0, concat_axis=0, tiled=True
    )
    stream_cols = unpack_units(recv_table, moved).reshape(tok_group, columns)
    stream_cols, cot_full = lax.optimization_barrier((stream_cols, cot_full))
    stream_full = lax.all_gather(stream_cols, "tensor", axis=1, tiled=True)

    grad_hidden = lax.dot_general(
        cot_full, down_weight, (((1,), (1,)), ((), ())), preferred_element_type=jnp.float32
    )
    cot_parts = deal(cot_full, share)
    stream_full, grad_hidden, *cot_parts = after(stream_full, grad_hidden, *cot_parts)
    cot_all = jnp.concatenate(cot_parts, axis=0)

    stream_f = stream_full.astype(jnp.float32)
    scaled_full = (stream_f * pick_gains(lang_tokens, norm_gains)).astype(jnp.bfloat16)
    inv_rms = lax.rsqrt(jnp.sum(stream_f * stream_f, axis=1) / width_d + 1e-05)

    my_start = lax.axis_index("tensor") * rows_here
    stream_rows = lax.dynamic_slice_in_dim(stream_full, my_start, rows_here, 0).astype(jnp.float32)
    lang_rows = lax.dynamic_slice_in_dim(lang_tokens, my_start, rows_here)
    gain_rows = pick_gains(lang_rows, norm_gains)
    scaled_rows = (stream_rows * gain_rows).astype(jnp.bfloat16)
    rms_rows = lax.dynamic_slice_in_dim(inv_rms, my_start, rows_here, 0)

    gate_acc = jnp.dot(scaled_full, gate_weight, preferred_element_type=jnp.float32)
    scaled_up, *dealt = after(scaled_full, *deal(scaled_rows, share))
    gathered = lax.all_gather(jnp.stack(dealt, axis=0), "tensor", axis=0)
    up_acc = jnp.dot(scaled_up, up_weight, preferred_element_type=jnp.float32)
    act_gate = inv_rms[:, None] * gate_acc
    act_up = inv_rms[:, None] * up_acc
    sigma = jax.nn.sigmoid(act_gate)
    silu = act_gate * sigma
    hidden = (silu * act_up).astype(jnp.bfloat16)
    weighted = inv_rms[:, None] * grad_hidden
    grad_gate = (weighted * act_up * sigma * (1.0 + act_gate * (1.0 - sigma))).astype(jnp.bfloat16)
    grad_up = (weighted * silu).astype(jnp.bfloat16)

    def over_tokens(left, right):
        return lax.dot_general(
            left, right, (((0,), (0,)), ((), ())), preferred_element_type=jnp.float32
        ).astype(jnp.bfloat16)

    def times_transposed(left, weight):
        return lax.dot_general(
            left, weight, (((1,), (1,)), ((), ())), preferred_element_type=jnp.float32
        )

    def scatter_rows(part):
        return lax.psum_scatter(
            part.astype(jnp.bfloat16), "tensor", scatter_dimension=0, tiled=True
        ).astype(jnp.float32)

    hidden_near = first_hops(hidden)
    out_part = jnp.dot(hidden, down_weight, preferred_element_type=jnp.float32)
    out_part, gathered = after(out_part, gathered)
    out_total = scatter_rows(out_part)
    scaled_all = gathered.transpose(1, 0, 2, 3).reshape(groups * tok_group, share)
    back_gate = times_transposed(grad_gate, gate_weight)

    grad_gate, grad_up, back_gate, *hidden_near = after(grad_gate, grad_up, back_gate, *hidden_near)
    gate_near = first_hops(grad_gate)
    hidden_far = second_hops(hidden_near)
    back_total = scatter_rows(back_gate + times_transposed(grad_up, up_weight))

    grad_up, *gate_near = after(grad_up, *gate_near)
    up_near = first_hops(grad_up)
    gate_far = second_hops(gate_near)
    down_grad = over_tokens(jnp.concatenate([hidden, *hidden_near, *hidden_far], axis=0), cot_all)

    up_near = after(*up_near)
    up_far = second_hops(up_near)
    gate_grad = over_tokens(scaled_all, jnp.concatenate([grad_gate, *gate_near, *gate_far], axis=0))
    up_grad = over_tokens(scaled_all, jnp.concatenate([grad_up, *up_near, *up_far], axis=0))

    layer_out = (stream_rows + out_total).astype(jnp.bfloat16)
    dot_sum = jnp.sum(scaled_rows.astype(jnp.float32) * back_total, axis=1)
    input_grad = (
        out_cotangent.astype(jnp.float32)
        + gain_rows * back_total
        - (rms_rows * rms_rows / width_d)[:, None] * stream_rows * dot_sum[:, None]
    ).astype(jnp.bfloat16)
    return (layer_out, input_grad, gate_grad, up_grad, down_grad)


def solution(mesh):
    return jax.shard_map(
        per_device,
        mesh=mesh,
        in_specs=(
            P("dp", "tensor"),
            P("dp", "tensor"),
            P("dp", "tensor"),
            P("dp", "tensor"),
            P(),
            P(),
            P(),
            P(),
            P(None, "tensor"),
            P(None, "tensor"),
            P("tensor", None),
            P(("dp", "tensor"), None),
        ),
        out_specs=(
            P(("dp", "tensor"), None),
            P(("dp", "tensor"), None),
            P("dp", "tensor"),
            P("dp", "tensor"),
            P("tensor", "dp"),
        ),
        check_vma=False,
    )
```

```python
import math

import jax
import jax.numpy as jnp
from jax import lax
from jax.sharding import PartitionSpec as P

HD = 128
UNIT = 48
CAP = 2
WIN = 24


def doc_index(doc_lengths, unit_len):
    doc_ends = jnp.cumsum(doc_lengths, axis=1)
    positions = jnp.arange(unit_len, dtype=jnp.int32)
    return jnp.sum((doc_ends[:, None, :] <= positions[None, :, None]).astype(jnp.int32), axis=2)


def attend(query_units, key_units, value_units, resid_units, doc_units):
    unit_count, unit_len, columns = query_units.shape
    head_shape = (unit_count, unit_len, columns // HD, HD)
    scores = jnp.einsum(
        "uqhd,ukhd->uhqk",
        query_units.reshape(head_shape),
        key_units.reshape(head_shape),
        preferred_element_type=jnp.float32,
    ) / math.sqrt(HD)
    positions = jnp.arange(unit_len, dtype=jnp.int32)
    distance = positions[:, None] - positions[None, :]
    allowed = (doc_units[:, :, None] == doc_units[:, None, :]) & (
        (distance >= 0) & (distance < WIN)
    )[None]
    scores = jnp.where(allowed[:, None], scores, -1e30)
    row_max = jnp.max(scores, axis=3, keepdims=True)
    exp_scores = jnp.exp(scores - row_max)
    attn_probs = (exp_scores / jnp.sum(exp_scores, axis=3, keepdims=True)).astype(jnp.bfloat16)
    mixed_heads = jnp.einsum(
        "uhqk,ukhd->uqhd",
        attn_probs,
        value_units.reshape(head_shape),
        preferred_element_type=jnp.float32,
    )
    return (
        resid_units.astype(jnp.float32) + mixed_heads.reshape(unit_count, unit_len, columns)
    ).astype(jnp.bfloat16)


def pack_units(send_table, unit_data):
    return jnp.einsum(
        "tsu,uic->tsic", send_table, unit_data, preferred_element_type=jnp.float32
    ).astype(jnp.bfloat16)


def unpack_units(recv_table, arrived):
    return jnp.einsum(
        "jts,tsic->jic", recv_table, arrived, preferred_element_type=jnp.float32
    ).astype(jnp.bfloat16)


def exchange(block, distance):
    groups = lax.axis_size("dp")
    return lax.ppermute(block, "dp", [(i, i ^ distance) for i in range(groups)])


def first_hops(block):
    groups = lax.axis_size("dp")
    distances = (1, 2) if groups == 4 else range(1, groups)
    return [exchange(block, o) for o in distances]


def far_halves(arrived):
    if lax.axis_size("dp") != 4:
        return []
    half = arrived[0].shape[0] // 2
    return [arrived[0][:half], arrived[1][half:]]


def second_hops(halves):
    return [exchange(half, 2 - index) for index, half in enumerate(halves)]


def after(value, *earlier):
    return lax.optimization_barrier((value, *earlier))


def deal(block, share):
    groups = lax.axis_size("dp")
    me = lax.axis_index("dp")
    parts = []
    for o in range(groups):
        piece = lax.dynamic_slice_in_dim(block, (me ^ o) * share, share, 1)
        parts.append(piece if o == 0 else exchange(piece, o))
    return parts


def pick_gains(langs, norm_gains):
    gains = jnp.zeros((langs.shape[0], norm_gains.shape[1]), jnp.float32)
    for index in range(norm_gains.shape[0]):
        gains = jnp.where((langs == index)[:, None], norm_gains[index][None, :], gains)
    return gains


def over_tokens(left, right):
    return lax.dot_general(
        left, right, (((0,), (0,)), ((), ())), preferred_element_type=jnp.float32
    )


def times_transposed(left, weight):
    return lax.dot_general(
        left, weight, (((1,), (1,)), ((), ())), preferred_element_type=jnp.float32
    )


def scatter_rows(part):
    return lax.psum_scatter(
        part, "tensor", scatter_dimension=0, tiled=True
    ).astype(jnp.float32)


def per_device(
    query_states,
    key_states,
    value_states,
    residual,
    norm_gains,
    lang_labels,
    doc_lengths,
    destinations,
    gate_weight,
    up_weight,
    down_weight,
    out_cotangent,
):
    groups = lax.axis_size("dp")
    shards = lax.axis_size("tensor")
    my_group = lax.axis_index("dp")
    total_units = destinations.shape[0]
    per_group = total_units // groups
    columns = query_states.shape[1]
    width_d = gate_weight.shape[0]
    share = width_d // groups
    tok_group = per_group * UNIT
    rows_here = out_cotangent.shape[0]
    first_unit = my_group * per_group

    half_rows = rows_here // 2
    cot_first = lax.all_gather(out_cotangent[:half_rows], "tensor", axis=0, tiled=True)

    own_docs = doc_index(lax.dynamic_slice_in_dim(doc_lengths, first_unit, per_group), UNIT)
    unit_shape = (per_group, UNIT, columns)
    mixed_units = attend(
        query_states.reshape(unit_shape),
        key_states.reshape(unit_shape),
        value_states.reshape(unit_shape),
        residual.reshape(unit_shape),
        own_docs,
    )

    unit_index = jnp.arange(total_units, dtype=jnp.int32)
    source_group = unit_index // per_group
    earlier = unit_index[None, :] < unit_index[:, None]
    same_target = destinations[None, :] == destinations[:, None]
    same_source = source_group[None, :] == source_group[:, None]
    send_rank = jnp.sum((earlier & same_target & same_source).astype(jnp.int32), axis=1)
    arrival = jnp.sum((earlier & same_target).astype(jnp.int32), axis=1)
    own_targets = lax.dynamic_slice_in_dim(destinations, first_unit, per_group)
    own_ranks = lax.dynamic_slice_in_dim(send_rank, first_unit, per_group)
    group_ids = jnp.arange(groups, dtype=jnp.int32)
    slot_ids = jnp.arange(CAP, dtype=jnp.int32)
    send_table = (
        (own_targets[None, None, :] == group_ids[:, None, None])
        & (own_ranks[None, None, :] == slot_ids[None, :, None])
    ).astype(jnp.bfloat16)
    arrive_ids = jnp.arange(per_group, dtype=jnp.int32)
    landing = (destinations == my_group)[None, :] & (arrival[None, :] == arrive_ids[:, None])
    recv_table = jnp.sum(
        (
            landing[:, None, None, :]
            & (source_group[None, None, None, :] == group_ids[None, :, None, None])
            & (send_rank[None, None, None, :] == slot_ids[None, None, :, None])
        ).astype(jnp.int32),
        axis=3,
    ).astype(jnp.bfloat16)
    moved_langs = jnp.sum(landing.astype(jnp.int32) * lang_labels[None, :], axis=1)
    lang_tokens = jnp.broadcast_to(moved_langs[:, None], (per_group, UNIT)).reshape(tok_group)

    moved = lax.all_to_all(
        pack_units(send_table, mixed_units), "dp", split_axis=0, concat_axis=0, tiled=True
    )
    stream_cols = unpack_units(recv_table, moved).reshape(tok_group, columns)
    stream_cols, cot_first = after(stream_cols, cot_first)
    stream_full = lax.all_gather(stream_cols, "tensor", axis=1, tiled=True)

    hidden_first = times_transposed(cot_first, down_weight)
    dealt_first = deal(cot_first, share)
    stream_full, hidden_first, last_rows, *dealt_first = after(
        stream_full, hidden_first, out_cotangent[half_rows:], *dealt_first
    )
    cot_last = lax.all_gather(last_rows, "tensor", axis=0, tiled=True)

    def interleave(first, last):
        shape = (shards, -1, first.shape[1])
        return jnp.concatenate([first.reshape(shape), last.reshape(shape)], axis=1).reshape(
            tok_group, first.shape[1]
        )

    stream_f = stream_full.astype(jnp.float32)
    scaled_full = (stream_f * pick_gains(lang_tokens, norm_gains)).astype(jnp.bfloat16)
    inv_rms = lax.rsqrt(jnp.sum(stream_f * stream_f, axis=1) / width_d + 1e-05)

    my_start = lax.axis_index("tensor") * rows_here
    stream_rows = lax.dynamic_slice_in_dim(stream_full, my_start, rows_here, 0).astype(jnp.float32)
    lang_rows = lax.dynamic_slice_in_dim(lang_tokens, my_start, rows_here)
    gain_rows = pick_gains(lang_rows, norm_gains)
    scaled_rows = (stream_rows * gain_rows).astype(jnp.bfloat16)
    rms_rows = lax.dynamic_slice_in_dim(inv_rms, my_start, rows_here, 0)

    gate_acc = jnp.dot(scaled_full, gate_weight, preferred_element_type=jnp.float32)
    scaled_up, *dealt = after(scaled_full, *deal(scaled_rows, share))
    gathered = lax.all_gather(jnp.stack(dealt, axis=0), "tensor", axis=0)
    up_acc = jnp.dot(scaled_up, up_weight, preferred_element_type=jnp.float32)
    act_gate = inv_rms[:, None] * gate_acc
    act_up = inv_rms[:, None] * up_acc
    dealt_last = deal(cot_last, share)
    hidden_last = times_transposed(cot_last, down_weight)
    grad_hidden = interleave(hidden_first, hidden_last)
    sigma = jax.nn.sigmoid(act_gate)
    silu = act_gate * sigma
    hidden = (silu * act_up).astype(jnp.bfloat16)
    weighted = inv_rms[:, None] * grad_hidden
    grad_gate = (weighted * act_up * sigma * (1.0 + act_gate * (1.0 - sigma))).astype(jnp.bfloat16)
    grad_up = (weighted * silu).astype(jnp.bfloat16)

    hidden, *dealt_last = after(hidden, *dealt_last)
    hidden_near = first_hops(hidden)
    out_part = jnp.dot(hidden, down_weight, preferred_element_type=jnp.float32)
    out_part = out_part.astype(jnp.bfloat16)

    grad_gate, grad_up, out_part, *hidden_near = after(grad_gate, grad_up, out_part, *hidden_near)
    halves = far_halves(hidden_near)
    gate_near = first_hops(grad_gate)
    hidden_far = second_hops(halves)
    back_part = times_transposed(grad_gate, gate_weight)
    back_part = (back_part + times_transposed(grad_up, up_weight)).astype(jnp.bfloat16)
    out_part, gathered = after(out_part, gathered)
    out_total = scatter_rows(out_part)
    grad_gate, grad_up, back_part, gathered, *rest = after(
        grad_gate, grad_up, back_part, gathered, *gate_near, *hidden_far, *dealt_first,
        *dealt_last
    )
    near_count, far_count = len(gate_near), len(hidden_far)
    gate_near, rest = rest[:near_count], rest[near_count:]
    hidden_far, rest = rest[:far_count], rest[far_count:]
    back_total = scatter_rows(back_part)
    scaled_all = gathered.transpose(1, 0, 2, 3).reshape(groups * tok_group, share)
    halves = far_halves(gate_near)
    up_near = first_hops(grad_up)
    gate_far = second_hops(halves)
    hidden_all = jnp.concatenate([hidden, *hidden_near, *hidden_far], axis=0)
    cot_all = jnp.concatenate(
        [interleave(*pair) for pair in zip(rest[:groups], rest[groups:])], axis=0
    )
    down_grad = over_tokens(hidden_all, cot_all)
    down_grad = down_grad.astype(jnp.bfloat16)

    _, *rest = after(down_grad[:8], *up_near, *gate_far)
    up_near, gate_far = rest[:near_count], rest[near_count:]
    halves = far_halves(up_near)
    up_far = second_hops(halves)
    gate_all = jnp.concatenate([grad_gate, *gate_near, *gate_far], axis=0)
    gate_grad = over_tokens(scaled_all, gate_all)
    gate_grad = gate_grad.astype(jnp.bfloat16)
    up_now = jnp.concatenate([grad_up, *up_near], axis=0)
    near_rows = up_now.shape[0]
    up_sum = over_tokens(scaled_all[:near_rows], up_now)
    if up_far:
        up_sum, _, *up_far = after(up_sum, gate_grad[:8], *up_far)
        up_sum = up_sum + over_tokens(scaled_all[near_rows:], jnp.concatenate(up_far, axis=0))
    up_grad = up_sum.astype(jnp.bfloat16)

    layer_out = (stream_rows + out_total).astype(jnp.bfloat16)
    dot_sum = jnp.sum(scaled_rows.astype(jnp.float32) * back_total, axis=1)
    input_grad = (
        out_cotangent.astype(jnp.float32)
        + gain_rows * back_total
        - (rms_rows * rms_rows / width_d)[:, None] * stream_rows * dot_sum[:, None]
    ).astype(jnp.bfloat16)
    return (layer_out, input_grad, gate_grad, up_grad, down_grad)


def solution(mesh):
    return jax.shard_map(
        per_device,
        mesh=mesh,
        in_specs=(
            P("dp", "tensor"),
            P("dp", "tensor"),
            P("dp", "tensor"),
            P("dp", "tensor"),
            P(),
            P(),
            P(),
            P(),
            P(None, "tensor"),
            P(None, "tensor"),
            P("tensor", None),
            P(("dp", "tensor"), None),
        ),
        out_specs=(
            P(("dp", "tensor"), None),
            P(("dp", "tensor"), None),
            P("dp", "tensor"),
            P("dp", "tensor"),
            P("tensor", "dp"),
        ),
        check_vma=False,
    )
```

```python
import math

import jax
import jax.numpy as jnp
from jax import lax
from jax.sharding import PartitionSpec as P

HD = 128
UNIT = 48
CAP = 2
WIN = 24


def doc_index(doc_lengths, unit_len):
    doc_ends = jnp.cumsum(doc_lengths, axis=1)
    positions = jnp.arange(unit_len, dtype=jnp.int32)
    return jnp.sum((doc_ends[:, None, :] <= positions[None, :, None]).astype(jnp.int32), axis=2)


def attend(query_units, key_units, value_units, resid_units, doc_units):
    unit_count, unit_len, columns = query_units.shape
    head_shape = (unit_count, unit_len, columns // HD, HD)
    scores = jnp.einsum(
        "uqhd,ukhd->uhqk",
        query_units.reshape(head_shape),
        key_units.reshape(head_shape),
        preferred_element_type=jnp.float32,
    ) / math.sqrt(HD)
    positions = jnp.arange(unit_len, dtype=jnp.int32)
    distance = positions[:, None] - positions[None, :]
    allowed = (doc_units[:, :, None] == doc_units[:, None, :]) & (
        (distance >= 0) & (distance < WIN)
    )[None]
    scores = jnp.where(allowed[:, None], scores, -1e30)
    row_max = jnp.max(scores, axis=3, keepdims=True)
    exp_scores = jnp.exp(scores - row_max)
    attn_probs = (exp_scores / jnp.sum(exp_scores, axis=3, keepdims=True)).astype(jnp.bfloat16)
    mixed_heads = jnp.einsum(
        "uhqk,ukhd->uqhd",
        attn_probs,
        value_units.reshape(head_shape),
        preferred_element_type=jnp.float32,
    )
    return (
        resid_units.astype(jnp.float32) + mixed_heads.reshape(unit_count, unit_len, columns)
    ).astype(jnp.bfloat16)


def pack_units(send_table, unit_data):
    return jnp.einsum(
        "tsu,uic->tsic", send_table, unit_data, preferred_element_type=jnp.float32
    ).astype(jnp.bfloat16)


def unpack_units(recv_table, arrived):
    return jnp.einsum(
        "jts,tsic->jic", recv_table, arrived, preferred_element_type=jnp.float32
    ).astype(jnp.bfloat16)


def exchange(block, distance):
    groups = lax.axis_size("dp")
    return lax.ppermute(block, "dp", [(i, i ^ distance) for i in range(groups)])


def first_hops(block):
    groups = lax.axis_size("dp")
    distances = (1, 2) if groups == 4 else range(1, groups)
    return [exchange(block, o) for o in distances]


def far_halves(arrived):
    if lax.axis_size("dp") != 4:
        return []
    half = arrived[0].shape[0] // 2
    return [arrived[0][:half], arrived[1][half:]]


def second_hops(halves):
    return [exchange(half, 2 - index) for index, half in enumerate(halves)]


def after(value, *earlier):
    return lax.optimization_barrier((value, *earlier))


def deal(block, share):
    groups = lax.axis_size("dp")
    me = lax.axis_index("dp")
    parts = []
    for o in range(groups):
        piece = lax.dynamic_slice_in_dim(block, (me ^ o) * share, share, 1)
        parts.append(piece if o == 0 else exchange(piece, o))
    return parts


def pick_gains(langs, norm_gains):
    gains = jnp.zeros((langs.shape[0], norm_gains.shape[1]), jnp.float32)
    for index in range(norm_gains.shape[0]):
        gains = jnp.where((langs == index)[:, None], norm_gains[index][None, :], gains)
    return gains


def over_tokens(left, right):
    return lax.dot_general(
        left, right, (((0,), (0,)), ((), ())), preferred_element_type=jnp.float32
    )


def times_transposed(left, weight):
    return lax.dot_general(
        left, weight, (((1,), (1,)), ((), ())), preferred_element_type=jnp.float32
    )


def scatter_rows(part):
    return lax.psum_scatter(
        part, "tensor", scatter_dimension=0, tiled=True
    ).astype(jnp.float32)


def per_device(
    query_states,
    key_states,
    value_states,
    residual,
    norm_gains,
    lang_labels,
    doc_lengths,
    destinations,
    gate_weight,
    up_weight,
    down_weight,
    out_cotangent,
):
    groups = lax.axis_size("dp")
    shards = lax.axis_size("tensor")
    my_group = lax.axis_index("dp")
    total_units = destinations.shape[0]
    per_group = total_units // groups
    columns = query_states.shape[1]
    width_d = gate_weight.shape[0]
    share = width_d // groups
    tok_group = per_group * UNIT
    rows_here = out_cotangent.shape[0]
    first_unit = my_group * per_group

    cot_full = lax.all_gather(out_cotangent, "tensor", axis=0, tiled=True)

    own_docs = doc_index(lax.dynamic_slice_in_dim(doc_lengths, first_unit, per_group), UNIT)
    unit_shape = (per_group, UNIT, columns)
    mixed_units = attend(
        query_states.reshape(unit_shape),
        key_states.reshape(unit_shape),
        value_states.reshape(unit_shape),
        residual.reshape(unit_shape),
        own_docs,
    )

    unit_index = jnp.arange(total_units, dtype=jnp.int32)
    source_group = unit_index // per_group
    earlier = unit_index[None, :] < unit_index[:, None]
    same_target = destinations[None, :] == destinations[:, None]
    same_source = source_group[None, :] == source_group[:, None]
    send_rank = jnp.sum((earlier & same_target & same_source).astype(jnp.int32), axis=1)
    arrival = jnp.sum((earlier & same_target).astype(jnp.int32), axis=1)
    own_targets = lax.dynamic_slice_in_dim(destinations, first_unit, per_group)
    own_ranks = lax.dynamic_slice_in_dim(send_rank, first_unit, per_group)
    group_ids = jnp.arange(groups, dtype=jnp.int32)
    slot_ids = jnp.arange(CAP, dtype=jnp.int32)
    send_table = (
        (own_targets[None, None, :] == group_ids[:, None, None])
        & (own_ranks[None, None, :] == slot_ids[None, :, None])
    ).astype(jnp.bfloat16)
    arrive_ids = jnp.arange(per_group, dtype=jnp.int32)
    landing = (destinations == my_group)[None, :] & (arrival[None, :] == arrive_ids[:, None])
    recv_table = jnp.sum(
        (
            landing[:, None, None, :]
            & (source_group[None, None, None, :] == group_ids[None, :, None, None])
            & (send_rank[None, None, None, :] == slot_ids[None, None, :, None])
        ).astype(jnp.int32),
        axis=3,
    ).astype(jnp.bfloat16)
    moved_langs = jnp.sum(landing.astype(jnp.int32) * lang_labels[None, :], axis=1)
    lang_tokens = jnp.broadcast_to(moved_langs[:, None], (per_group, UNIT)).reshape(tok_group)

    moved = lax.all_to_all(
        pack_units(send_table, mixed_units), "dp", split_axis=0, concat_axis=0, tiled=True
    )
    stream_cols = unpack_units(recv_table, moved).reshape(tok_group, columns)
    stream_cols, cot_full = after(stream_cols, cot_full)
    stream_full = lax.all_gather(stream_cols, "tensor", axis=1, tiled=True)

    grad_hidden = times_transposed(cot_full, down_weight)
    cot_parts = deal(cot_full, share)
    stream_full, grad_hidden, *cot_parts = after(stream_full, grad_hidden, *cot_parts)
    cot_all = jnp.concatenate(cot_parts, axis=0)

    stream_f = stream_full.astype(jnp.float32)
    scaled_full = (stream_f * pick_gains(lang_tokens, norm_gains)).astype(jnp.bfloat16)
    inv_rms = lax.rsqrt(jnp.sum(stream_f * stream_f, axis=1) / width_d + 1e-05)

    my_start = lax.axis_index("tensor") * rows_here
    stream_rows = lax.dynamic_slice_in_dim(stream_full, my_start, rows_here, 0).astype(jnp.float32)
    lang_rows = lax.dynamic_slice_in_dim(lang_tokens, my_start, rows_here)
    gain_rows = pick_gains(lang_rows, norm_gains)
    scaled_rows = (stream_rows * gain_rows).astype(jnp.bfloat16)
    rms_rows = lax.dynamic_slice_in_dim(inv_rms, my_start, rows_here, 0)

    gate_acc = jnp.dot(scaled_full, gate_weight, preferred_element_type=jnp.float32)
    up_acc = jnp.dot(scaled_full, up_weight, preferred_element_type=jnp.float32)
    act_gate = inv_rms[:, None] * gate_acc
    act_up = inv_rms[:, None] * up_acc
    sigma = jax.nn.sigmoid(act_gate)
    silu = act_gate * sigma
    hidden = (silu * act_up).astype(jnp.bfloat16)
    weighted = inv_rms[:, None] * grad_hidden
    grad_gate = (weighted * act_up * sigma * (1.0 + act_gate * (1.0 - sigma))).astype(jnp.bfloat16)
    grad_up = (weighted * silu).astype(jnp.bfloat16)

    hidden_near = first_hops(hidden)
    near_count = len(hidden_near)
    dealt = deal(scaled_rows, share)
    out_part = jnp.dot(hidden, down_weight, preferred_element_type=jnp.float32)
    out_part = out_part.astype(jnp.bfloat16)

    grad_gate, grad_up, out_part, *rest = after(grad_gate, grad_up, out_part, *hidden_near, *dealt)
    hidden_near, dealt = rest[:near_count], rest[near_count:]
    gathered = lax.all_gather(jnp.stack(dealt, axis=0), "tensor", axis=0)
    out_total = scatter_rows(out_part)
    gate_near = first_hops(grad_gate)
    hidden_far = second_hops(far_halves(hidden_near))
    far_count = len(hidden_far)
    back_part = times_transposed(grad_gate, gate_weight)
    back_part = (back_part + times_transposed(grad_up, up_weight)).astype(jnp.bfloat16)

    grad_up, back_part, *rest = after(grad_up, back_part, *gate_near, *hidden_far)
    gate_near, hidden_far = rest[:near_count], rest[near_count:]
    up_near = first_hops(grad_up)
    gate_far = second_hops(far_halves(gate_near))
    back_total = scatter_rows(back_part)
    hidden, gathered, out_total = after(hidden, gathered, out_total)
    down_grad = over_tokens(
        jnp.concatenate([hidden, *hidden_near, *hidden_far], axis=0), cot_all
    ).astype(jnp.bfloat16)

    down_grad, *rest = after(down_grad, *up_near, *gate_far)
    up_near, gate_far = rest[:near_count], rest[near_count:]
    up_far = second_hops(far_halves(up_near))
    scaled_all = gathered.transpose(1, 0, 2, 3).reshape(groups * tok_group, share)
    gate_grad = over_tokens(
        scaled_all, jnp.concatenate([grad_gate, *gate_near, *gate_far], axis=0)
    ).astype(jnp.bfloat16)
    up_grad = over_tokens(
        scaled_all, jnp.concatenate([grad_up, *up_near, *up_far], axis=0)
    ).astype(jnp.bfloat16)

    layer_out = (stream_rows + out_total).astype(jnp.bfloat16)
    dot_sum = jnp.sum(scaled_rows.astype(jnp.float32) * back_total, axis=1)
    input_grad = (
        out_cotangent.astype(jnp.float32)
        + gain_rows * back_total
        - (rms_rows * rms_rows / width_d)[:, None] * stream_rows * dot_sum[:, None]
    ).astype(jnp.bfloat16)
    return (layer_out, input_grad, gate_grad, up_grad, down_grad)


def solution(mesh):
    return jax.shard_map(
        per_device,
        mesh=mesh,
        in_specs=(
            P("dp", "tensor"),
            P("dp", "tensor"),
            P("dp", "tensor"),
            P("dp", "tensor"),
            P(),
            P(),
            P(),
            P(),
            P(None, "tensor"),
            P(None, "tensor"),
            P("tensor", None),
            P(("dp", "tensor"), None),
        ),
        out_specs=(
            P(("dp", "tensor"), None),
            P(("dp", "tensor"), None),
            P("dp", "tensor"),
            P("dp", "tensor"),
            P("tensor", "dp"),
        ),
        check_vma=False,
    )
```

```python
import math

import jax
import jax.numpy as jnp
from jax import lax
from jax.sharding import PartitionSpec as P

HD = 128
UNIT = 48
CAP = 2
WIN = 24


def doc_index(doc_lengths, unit_len):
    doc_ends = jnp.cumsum(doc_lengths, axis=1)
    positions = jnp.arange(unit_len, dtype=jnp.int32)
    return jnp.sum((doc_ends[:, None, :] <= positions[None, :, None]).astype(jnp.int32), axis=2)


def attend(query_units, key_units, value_units, resid_units, doc_units):
    unit_count, unit_len, columns = query_units.shape
    head_shape = (unit_count, unit_len, columns // HD, HD)
    scores = jnp.einsum(
        "uqhd,ukhd->uhqk",
        query_units.reshape(head_shape),
        key_units.reshape(head_shape),
        preferred_element_type=jnp.float32,
    ) / math.sqrt(HD)
    positions = jnp.arange(unit_len, dtype=jnp.int32)
    distance = positions[:, None] - positions[None, :]
    allowed = (doc_units[:, :, None] == doc_units[:, None, :]) & (
        (distance >= 0) & (distance < WIN)
    )[None]
    scores = jnp.where(allowed[:, None], scores, -1e30)
    row_max = jnp.max(scores, axis=3, keepdims=True)
    exp_scores = jnp.exp(scores - row_max)
    attn_probs = (exp_scores / jnp.sum(exp_scores, axis=3, keepdims=True)).astype(jnp.bfloat16)
    mixed_heads = jnp.einsum(
        "uhqk,ukhd->uqhd",
        attn_probs,
        value_units.reshape(head_shape),
        preferred_element_type=jnp.float32,
    )
    return (
        resid_units.astype(jnp.float32) + mixed_heads.reshape(unit_count, unit_len, columns)
    ).astype(jnp.bfloat16)


def pack_units(send_table, unit_data):
    return jnp.einsum(
        "tsu,uic->tsic", send_table, unit_data, preferred_element_type=jnp.float32
    ).astype(jnp.bfloat16)


def unpack_units(recv_table, arrived):
    return jnp.einsum(
        "jts,tsic->jic", recv_table, arrived, preferred_element_type=jnp.float32
    ).astype(jnp.bfloat16)


def exchange(block, distance):
    groups = lax.axis_size("dp")
    return lax.ppermute(block, "dp", [(i, i ^ distance) for i in range(groups)])


def first_hops(block):
    groups = lax.axis_size("dp")
    distances = (1, 2) if groups == 4 else range(1, groups)
    return [exchange(block, o) for o in distances]


def far_halves(arrived):
    if lax.axis_size("dp") != 4:
        return []
    half = arrived[0].shape[0] // 2
    return [arrived[0][:half], arrived[1][half:]]


def second_hops(halves):
    return [exchange(half, 2 - index) for index, half in enumerate(halves)]


def after(value, *earlier):
    return lax.optimization_barrier((value, *earlier))


def deal(block, share):
    groups = lax.axis_size("dp")
    me = lax.axis_index("dp")
    parts = []
    for o in range(groups):
        piece = lax.dynamic_slice_in_dim(block, (me ^ o) * share, share, 1)
        parts.append(piece if o == 0 else exchange(piece, o))
    return parts


def pick_gains(langs, norm_gains):
    gains = jnp.zeros((langs.shape[0], norm_gains.shape[1]), jnp.float32)
    for index in range(norm_gains.shape[0]):
        gains = jnp.where((langs == index)[:, None], norm_gains[index][None, :], gains)
    return gains


def over_tokens(left, right):
    return lax.dot_general(
        left, right, (((0,), (0,)), ((), ())), preferred_element_type=jnp.float32
    )


def times_transposed(left, weight):
    return lax.dot_general(
        left, weight, (((1,), (1,)), ((), ())), preferred_element_type=jnp.float32
    )


def scatter_rows(part):
    return lax.psum_scatter(
        part, "tensor", scatter_dimension=0, tiled=True
    ).astype(jnp.float32)


def per_device(
    query_states,
    key_states,
    value_states,
    residual,
    norm_gains,
    lang_labels,
    doc_lengths,
    destinations,
    gate_weight,
    up_weight,
    down_weight,
    out_cotangent,
):
    groups = lax.axis_size("dp")
    shards = lax.axis_size("tensor")
    my_group = lax.axis_index("dp")
    total_units = destinations.shape[0]
    per_group = total_units // groups
    columns = query_states.shape[1]
    width_d = gate_weight.shape[0]
    share = width_d // groups
    tok_group = per_group * UNIT
    rows_here = out_cotangent.shape[0]
    first_unit = my_group * per_group

    cot_full = lax.all_gather(out_cotangent, "tensor", axis=0, tiled=True)

    own_docs = doc_index(lax.dynamic_slice_in_dim(doc_lengths, first_unit, per_group), UNIT)
    unit_shape = (per_group, UNIT, columns)
    mixed_units = attend(
        query_states.reshape(unit_shape),
        key_states.reshape(unit_shape),
        value_states.reshape(unit_shape),
        residual.reshape(unit_shape),
        own_docs,
    )

    unit_index = jnp.arange(total_units, dtype=jnp.int32)
    source_group = unit_index // per_group
    earlier = unit_index[None, :] < unit_index[:, None]
    same_target = destinations[None, :] == destinations[:, None]
    same_source = source_group[None, :] == source_group[:, None]
    send_rank = jnp.sum((earlier & same_target & same_source).astype(jnp.int32), axis=1)
    arrival = jnp.sum((earlier & same_target).astype(jnp.int32), axis=1)
    own_targets = lax.dynamic_slice_in_dim(destinations, first_unit, per_group)
    own_ranks = lax.dynamic_slice_in_dim(send_rank, first_unit, per_group)
    group_ids = jnp.arange(groups, dtype=jnp.int32)
    slot_ids = jnp.arange(CAP, dtype=jnp.int32)
    send_table = (
        (own_targets[None, None, :] == group_ids[:, None, None])
        & (own_ranks[None, None, :] == slot_ids[None, :, None])
    ).astype(jnp.bfloat16)
    arrive_ids = jnp.arange(per_group, dtype=jnp.int32)
    landing = (destinations == my_group)[None, :] & (arrival[None, :] == arrive_ids[:, None])
    recv_table = jnp.sum(
        (
            landing[:, None, None, :]
            & (source_group[None, None, None, :] == group_ids[None, :, None, None])
            & (send_rank[None, None, None, :] == slot_ids[None, None, :, None])
        ).astype(jnp.int32),
        axis=3,
    ).astype(jnp.bfloat16)
    moved_langs = jnp.sum(landing.astype(jnp.int32) * lang_labels[None, :], axis=1)
    lang_tokens = jnp.broadcast_to(moved_langs[:, None], (per_group, UNIT)).reshape(tok_group)

    moved = lax.all_to_all(
        pack_units(send_table, mixed_units), "dp", split_axis=0, concat_axis=0, tiled=True
    )
    stream_cols = unpack_units(recv_table, moved).reshape(tok_group, columns)
    stream_cols, cot_full = after(stream_cols, cot_full)
    stream_full = lax.all_gather(stream_cols, "tensor", axis=1, tiled=True)

    grad_hidden = times_transposed(cot_full, down_weight)
    cot_parts = deal(cot_full, share)
    stream_full, grad_hidden, *cot_parts = after(stream_full, grad_hidden, *cot_parts)
    cot_all = jnp.concatenate(cot_parts, axis=0)

    stream_f = stream_full.astype(jnp.float32)
    scaled_full = (stream_f * pick_gains(lang_tokens, norm_gains)).astype(jnp.bfloat16)
    inv_rms = lax.rsqrt(jnp.sum(stream_f * stream_f, axis=1) / width_d + 1e-05)

    my_start = lax.axis_index("tensor") * rows_here
    stream_rows = lax.dynamic_slice_in_dim(stream_full, my_start, rows_here, 0).astype(jnp.float32)
    lang_rows = lax.dynamic_slice_in_dim(lang_tokens, my_start, rows_here)
    gain_rows = pick_gains(lang_rows, norm_gains)
    scaled_rows = (stream_rows * gain_rows).astype(jnp.bfloat16)
    rms_rows = lax.dynamic_slice_in_dim(inv_rms, my_start, rows_here, 0)

    gate_acc = jnp.dot(scaled_full, gate_weight, preferred_element_type=jnp.float32)
    scaled_up, *dealt = after(scaled_full, *deal(scaled_rows, share))
    gathered = lax.all_gather(jnp.stack(dealt, axis=0), "tensor", axis=0)
    up_acc = jnp.dot(scaled_up, up_weight, preferred_element_type=jnp.float32)
    act_gate = inv_rms[:, None] * gate_acc
    act_up = inv_rms[:, None] * up_acc
    sigma = jax.nn.sigmoid(act_gate)
    silu = act_gate * sigma
    hidden = (silu * act_up).astype(jnp.bfloat16)
    weighted = inv_rms[:, None] * grad_hidden
    grad_gate = (weighted * act_up * sigma * (1.0 + act_gate * (1.0 - sigma))).astype(jnp.bfloat16)
    grad_up = (weighted * silu).astype(jnp.bfloat16)

    hidden_near = first_hops(hidden)
    near_count = len(hidden_near)
    out_part = jnp.dot(hidden, down_weight, preferred_element_type=jnp.float32)
    out_part = out_part.astype(jnp.bfloat16)

    grad_gate, grad_up, out_part, *hidden_near = after(grad_gate, grad_up, out_part, *hidden_near)
    gate_near = first_hops(grad_gate)
    hidden_far = second_hops(far_halves(hidden_near))
    out_part, gathered = after(out_part, gathered)
    out_total = scatter_rows(out_part)
    back_part = times_transposed(grad_gate, gate_weight)
    back_part = (back_part + times_transposed(grad_up, up_weight)).astype(jnp.bfloat16)

    hidden, grad_up, back_part, *rest = after(hidden, grad_up, back_part, *gate_near, *hidden_far)
    gate_near, hidden_far = rest[:near_count], rest[near_count:]
    gate_far = second_hops(far_halves(gate_near))
    back_total = scatter_rows(back_part)
    down_grad = over_tokens(
        jnp.concatenate([hidden, *hidden_near, *hidden_far], axis=0), cot_all
    ).astype(jnp.bfloat16)

    grad_up, down_grad, out_total, *gate_far = after(grad_up, down_grad, out_total, *gate_far)
    up_near = first_hops(grad_up)
    scaled_all = gathered.transpose(1, 0, 2, 3).reshape(groups * tok_group, share)
    gate_grad = over_tokens(
        scaled_all, jnp.concatenate([grad_gate, *gate_near, *gate_far], axis=0)
    ).astype(jnp.bfloat16)

    gate_grad, *up_near = after(gate_grad, *up_near)
    up_far = second_hops(far_halves(up_near))
    scaled_rows, *up_far = after(scaled_rows, *up_far)
    up_grad = over_tokens(
        scaled_all, jnp.concatenate([grad_up, *up_near, *up_far], axis=0)
    ).astype(jnp.bfloat16)

    layer_out = (stream_rows + out_total).astype(jnp.bfloat16)
    dot_sum = jnp.sum(scaled_rows.astype(jnp.float32) * back_total, axis=1)
    input_grad = (
        out_cotangent.astype(jnp.float32)
        + gain_rows * back_total
        - (rms_rows * rms_rows / width_d)[:, None] * stream_rows * dot_sum[:, None]
    ).astype(jnp.bfloat16)
    return (layer_out, input_grad, gate_grad, up_grad, down_grad)


def solution(mesh):
    return jax.shard_map(
        per_device,
        mesh=mesh,
        in_specs=(
            P("dp", "tensor"),
            P("dp", "tensor"),
            P("dp", "tensor"),
            P("dp", "tensor"),
            P(),
            P(),
            P(),
            P(),
            P(None, "tensor"),
            P(None, "tensor"),
            P("tensor", None),
            P(("dp", "tensor"), None),
        ),
        out_specs=(
            P(("dp", "tensor"), None),
            P(("dp", "tensor"), None),
            P("dp", "tensor"),
            P("dp", "tensor"),
            P("tensor", "dp"),
        ),
        check_vma=False,
    )
```
